768 devices in a mesh: row: 96 (over z, x, core), col: 8 (over y).
Axes of the slice: x: 4, y: 8, z: 12, core: 2. Of those that a mesh axis runs over, the one named last changes fastest.
Arguments:
- ensemble: float32 [98304, 1024], P(('row', 'col')), may hold values from -6 to 6
- obs_blocks: int32 [2, 256], replicated, may hold values from 0 to 24575
- obs_weights: float32 [2, 256, 4], replicated, may hold values from 0.1 to 1
- comp_tags: int32 [2, 256], replicated, may hold values from 0 to 1
- obs_values: float32 [2, 256], replicated, may hold values from -6 to 6
- obs_noise: bfloat16 [2, 256, 1024], replicated, may hold values from -6 to 6
Outputs:
- analysis: float32 [98304, 1024], P(('row', 'col'))
The draws below stay inside these ranges and needn't reach their ends.
Inputs may be any that keep to these rules, and one draw needn't show every extreme that they name: Observation o reads state rows 4 * obs_blocks[b, o] to 4 * obs_blocks[b, o] + 3. `comp_tags`: 0 marks an atmosphere observation, 1 an ocean one.
All inputs are finite; a program needn't handle non-finite values.
Results may differ from the reference program's by a relative error of at most 0.0035.
Values may be sent and summed in bfloat16 or wider, within the bound.
A program may use at most 32 MiB of HBM per device.

```python
import jax
import jax.numpy as jnp
from jax import lax

M = 1024
B = 256
K = 4
NB = 2
NROWS = 98304
NBLK = 24576


def set_ends(values, rng, smallest, top_value):
    longest = values.shape.index(max(values.shape))
    spots = []
    for shift in (0, 1):
        where = [jax.random.randint(jax.random.fold_in(rng, axis), (), 0, length) for axis, length in enumerate(values.shape)]
        where[longest] = (where[longest] + shift) % values.shape[longest]
        spots.append(tuple(where))
    return values.at[spots[0]].set(smallest).at[spots[1]].set(top_value)


def block_scale(rng, shape, split, low, high):
    factor_of, own = 1.0, jax.random.fold_in(rng, 6)
    for position, blocks in split:
        draws = jnp.exp(jax.random.uniform(jax.random.fold_in(own, position), (blocks,), jnp.float32, low / len(split), high / len(split)))
        factor_of = factor_of * jnp.repeat(draws, shape[position] // blocks).reshape([-1 if axis == position else 1 for axis in range(len(shape))])
    return factor_of


def gaussian(own_key, extent, deviation, most, pieces=(), kind=jnp.bfloat16):
    values = deviation * jax.random.normal(own_key, extent, jnp.float32)
    if pieces:
        values = values * block_scale(own_key, extent, pieces, -0.22, 0.18)
    return jnp.clip(values, -most, most).astype(kind)


def setup_inputs(seed: int = 0) -> dict:
    arg_keys = jax.random.split(jax.random.key(seed), 7)
    ensemble = gaussian(arg_keys[0], (NROWS, M), 1.0, 6.0, ((0, 768),), jnp.float32)
    obs_blocks = set_ends(jax.random.randint(arg_keys[1], (NB, B), 0, NBLK), jax.random.fold_in(arg_keys[1], 1), 0, NBLK - 1).astype(jnp.int32)
    obs_weights = jnp.clip(jax.random.uniform(arg_keys[2], (NB, B, K), jnp.float32, 0.1, 1.0), 0.1, 1.0)
    comp_tags = set_ends(jax.random.randint(arg_keys[3], (NB, B), 0, 2), jax.random.fold_in(arg_keys[3], 1), 0, 1).astype(jnp.int32)
    obs_values = gaussian(arg_keys[4], (NB, B), 1.0, 6.0, (), jnp.float32)
    obs_noise = gaussian(arg_keys[5], (NB, B, M), 1.0, 6.0)
    return dict(ensemble=ensemble, obs_blocks=obs_blocks, obs_weights=obs_weights, comp_tags=comp_tags, obs_values=obs_values, obs_noise=obs_noise)


def reference(ensemble, obs_blocks, obs_weights, comp_tags, obs_values, obs_noise):
    ensemble_state = ensemble
    highest = lax.Precision.HIGHEST
    for batch_index in range(NB):
        row_ids = obs_blocks[batch_index][:, None] * K + jnp.arange(K, dtype=jnp.int32)[None, :]
        picked = ensemble_state[row_ids.reshape(-1)].reshape(B, K, M)
        observed = lax.optimization_barrier(jnp.sum(obs_weights[batch_index][:, :, None] * picked, axis=1))
        observed = lax.optimization_barrier(observed.astype(jnp.bfloat16)).astype(jnp.float32)
        anomalies = observed - lax.optimization_barrier(jnp.mean(observed, axis=1, keepdims=True))
        variance = jnp.where(comp_tags[batch_index] == 0, jnp.float32(0.5), jnp.float32(2.0))
        covariance = jnp.dot(anomalies, anomalies.T, precision=highest) / (M - 1) + jnp.diag(variance)
        factor_lower = jnp.linalg.cholesky(covariance)
        innovation = obs_values[batch_index][:, None] + jnp.sqrt(variance)[:, None] * obs_noise[batch_index].astype(jnp.float32) - observed
        whitened = jax.scipy.linalg.solve_triangular(factor_lower, anomalies, lower=True).astype(jnp.bfloat16)
        white_innov = jax.scipy.linalg.solve_triangular(factor_lower, innovation, lower=True).astype(jnp.bfloat16)
        state_anom = ensemble_state - lax.optimization_barrier(jnp.mean(ensemble_state, axis=1, keepdims=True))
        projected = jnp.dot(state_anom, whitened.astype(jnp.float32).T, precision=highest)
        ensemble_state = ensemble_state + jnp.dot(projected, white_innov.astype(jnp.float32), precision=highest) / (M - 1)
    return ensemble_state
```

```python
import functools

import jax
import jax.numpy as jnp
from jax import lax
from jax.experimental import pallas as pl
from jax.experimental.pallas import tpu as pltpu
from jax.sharding import PartitionSpec as P

NX = 4
TILE_ROWS = 16
TILE_COLS = 128
MESH = pl.DeviceIdType.MESH


def split(value):
    high = value.astype(jnp.bfloat16)
    return high, (value - high.astype(jnp.float32)).astype(jnp.bfloat16)


def dot_tn(left, right):
    return lax.dot_general(
        left, right, (((0,), (0,)), ((), ())), preferred_element_type=jnp.float32
    )


def gather_kernel(nz, nx, ny, state_ref, blocks_ref, weights_ref, out_ref, *scratch):
    nb = blocks_ref.shape[0]
    batches = [scratch[7 * b : 7 * b + 7] for b in range(nb)]
    send_sems, recv_sems = scratch[7 * nb :]
    row = lax.axis_index("row")
    y = lax.axis_index("col")
    core = lax.rem(row, 2)
    x = lax.rem(row // 2, nx)
    z = row // (2 * nx)

    def place(z_, x_, core_, y_):
        return ((z_ * nx + x_) * 2 + core_, y_)

    core_peer = place(z, x, 1 - core, y)
    x_peers = [place(z, lax.rem(x + d, nx), core, y) for d in range(1, nx)]
    y_peers = [place(z, x, core, lax.rem(y + d, ny)) for d in range(1, ny)]
    z_peers = [place(lax.rem(z + d, nz), x, core, y) for d in range(1, nz)]
    peers = [core_peer, *x_peers, *y_peers, *z_peers]

    barrier = pltpu.get_barrier_semaphore()
    for peer in peers:
        pl.semaphore_signal(barrier, inc=1, device_id=peer, device_id_type=MESH)

    def interpolate(b):
        part = batches[b][0]
        rows = state_ref.shape[0]
        state_high, state_low = split(state_ref[...])
        observations = blocks_ref.shape[1]
        position = lax.broadcasted_iota(jnp.int32, (rows, observations), 0)
        first = (row * ny + y) * (rows // 4)
        held = blocks_ref[b : b + 1, :] - first == position // 4
        within = lax.rem(position, 4)
        weights = jnp.zeros((rows, observations), jnp.float32)
        for k in range(4):
            weights = jnp.where(within == k, weights_ref[b, k : k + 1, :], weights)
        selector_high, selector_low = split(jnp.where(held, weights, 0.0))
        values = (
            dot_tn(selector_low, state_high)
            + dot_tn(selector_high, state_low)
            + dot_tn(selector_high, state_high)
        ).astype(jnp.bfloat16)
        tile = 0
        per_x = part.shape[1] // nx
        half = part.shape[1]
        for i in range(values.shape[0] // TILE_ROWS):
            for j in range(values.shape[1] // TILE_COLS):
                part[tile // half, tile % half] = values[
                    i * TILE_ROWS : (i + 1) * TILE_ROWS, j * TILE_COLS : (j + 1) * TILE_COLS
                ]
                tile += 1

    def copy(b, index, source, target, peer):
        return pltpu.make_async_remote_copy(
            src_ref=source,
            dst_ref=target,
            send_sem=send_sems.at[b, index],
            recv_sem=recv_sems.at[b, index],
            device_id=peer,
            device_id_type=MESH,
        )

    per_x = batches[0][0].shape[1] // nx
    per_y = per_x // ny
    base = [0]
    for count in (1, nx - 1, ny - 1, nz - 1, ny - 1, nx - 1, 1):
        base.append(base[-1] + count)

    def start_stage(b, stage):
        part, from_core, from_x, from_y, from_z, mine, full = batches[b]
        copies = []
        if stage == 0:
            copies.append(copy(b, 0, part.at[1 - core], from_core, core_peer))
        elif stage == 1:
            for d in range(1, nx):
                target = lax.rem(x + d, nx)
                source = part.at[core, pl.ds(target * per_x, per_x)]
                copies.append(copy(b, base[1] + d - 1, source, from_x.at[d - 1], x_peers[d - 1]))
        elif stage == 2:
            for d in range(1, ny):
                target = lax.rem(y + d, ny)
                source = part.at[core, pl.ds(x * per_x + target * per_y, per_y)]
                copies.append(copy(b, base[2] + d - 1, source, from_y.at[d - 1], y_peers[d - 1]))
        elif stage == 3:
            for d in range(1, nz):
                copies.append(copy(b, base[3] + d - 1, mine, from_z.at[d - 1], z_peers[d - 1]))
        elif stage == 4:
            whole = full.at[core, x, y]
            for d in range(1, ny):
                copies.append(copy(b, base[4] + d - 1, whole, whole, y_peers[d - 1]))
        elif stage == 5:
            whole = full.at[core, x]
            for d in range(1, nx):
                copies.append(copy(b, base[5] + d - 1, whole, whole, x_peers[d - 1]))
        else:
            whole = full.at[core]
            copies.append(copy(b, base[6], whole, whole, core_peer))
        for each in copies:
            each.start()
        return copies

    def finish_stage(b, stage, copies):
        part, from_core, from_x, from_y, from_z, mine, full = batches[b]
        for each in copies:
            each.wait_recv()
        if stage == 0:
            part[core] = part[core] + from_core[...]
        elif stage == 1:
            here = pl.ds(x * per_x, per_x)
            part[core, here] = part[core, here] + functools.reduce(
                jnp.add, [from_x[d] for d in range(nx - 1)]
            )
        elif stage == 2:
            here = pl.ds(x * per_x + y * per_y, per_y)
            mine[...] = part[core, here] + functools.reduce(
                jnp.add, [from_y[d] for d in range(ny - 1)]
            )
        elif stage == 3:
            full[core, x, y] = mine[...] + functools.reduce(
                jnp.add, [from_z[d] for d in range(nz - 1)]
            )

    started = [[] for _ in range(nb)]
    current = [None] * nb
    for b in range(nb):
        interpolate(b)
        if b == 0:
            pl.semaphore_wait(barrier, len(peers))
        current[b] = start_stage(b, 0)
        started[b] += current[b]
    for stage in range(7):
        for b in range(nb):
            finish_stage(b, stage, current[b])
            if stage < 6:
                current[b] = start_stage(b, stage + 1)
                started[b] += current[b]
    for b in range(nb):
        full = batches[b][6]
        columns = out_ref.shape[2] // TILE_COLS
        for i in range(out_ref.shape[1] // TILE_ROWS):
            for j in range(columns):
                tile = i * columns + j
                c, rest = divmod(tile, nx * per_x)
                x_, rest = divmod(rest, per_x)
                y_, t = divmod(rest, per_y)
                out_ref[
                    b, i * TILE_ROWS : (i + 1) * TILE_ROWS, j * TILE_COLS : (j + 1) * TILE_COLS
                ] = full[c, x_, y_, t]
    for b in range(nb):
        for each in started[b]:
            each.wait_send()


def gather_observed(ensemble, obs_blocks, obs_weights):
    nx = NX
    ny = lax.axis_size("col")
    nz = lax.axis_size("row") // (2 * nx)
    batches, observations = obs_blocks.shape
    members = ensemble.shape[1]
    tiles = observations * members // (TILE_ROWS * TILE_COLS)
    per_x = tiles // (2 * nx)
    per_y = per_x // ny
    tile = (TILE_ROWS, TILE_COLS)
    one_batch = [
        pltpu.VMEM((2, tiles // 2, *tile), jnp.bfloat16),
        pltpu.VMEM((tiles // 2, *tile), jnp.bfloat16),
        pltpu.VMEM((nx - 1, per_x, *tile), jnp.bfloat16),
        pltpu.VMEM((ny - 1, per_y, *tile), jnp.bfloat16),
        pltpu.VMEM((nz - 1, per_y, *tile), jnp.bfloat16),
        pltpu.VMEM((per_y, *tile), jnp.bfloat16),
        pltpu.VMEM((2, nx, ny, per_y, *tile), jnp.bfloat16),
    ]
    copies = 2 * (1 + nx - 1 + ny - 1) + nz - 1
    vmem = pl.BlockSpec(memory_space=pltpu.VMEM)
    return pl.pallas_call(
        functools.partial(gather_kernel, nz, nx, ny),
        out_shape=jax.ShapeDtypeStruct((batches, observations, members), jnp.bfloat16),
        in_specs=[vmem] * 3,
        out_specs=vmem,
        scratch_shapes=one_batch * batches
        + [
            pltpu.SemaphoreType.DMA((batches, copies)),
            pltpu.SemaphoreType.DMA((batches, copies)),
        ],
        compiler_params=pltpu.CompilerParams(
            collective_id=0, has_side_effects=True, vmem_limit_bytes=32 * 1024 * 1024
        ),
        cost_estimate=pl.CostEstimate(flops=10**8, bytes_accessed=10**7, transcendentals=0),
        name="gather_observed",
    )(ensemble, obs_blocks, jnp.transpose(obs_weights, (0, 2, 1)))


def body(ensemble, obs_blocks, obs_weights, comp_tags, obs_values, obs_noise):
    highest = lax.Precision.HIGHEST
    members = ensemble.shape[1]
    raw = gather_observed(ensemble, obs_blocks, obs_weights)
    state = ensemble
    pending = raw[1].astype(jnp.float32)
    observed = raw[0].astype(jnp.float32)
    for b in range(obs_blocks.shape[0]):
        anomalies = observed - jnp.mean(observed, axis=1, keepdims=True)
        variance = jnp.where(comp_tags[b] == 0, jnp.float32(0.5), jnp.float32(2.0))
        covariance = jnp.dot(anomalies, anomalies.T, precision=highest) / (members - 1) + jnp.diag(
            variance
        )
        factor_lower = jnp.linalg.cholesky(covariance)
        innovation = (
            obs_values[b][:, None]
            + jnp.sqrt(variance)[:, None] * obs_noise[b].astype(jnp.float32)
            - observed
        )
        stacked = jnp.concatenate([anomalies, innovation], axis=1)
        solved = jax.scipy.linalg.solve_triangular(factor_lower, stacked, lower=True).astype(
            jnp.bfloat16
        )
        whitened, white_innov = solved[:, :members], solved[:, members:]

        def update(value):
            centred = value - jnp.mean(value, axis=1, keepdims=True)
            projected = jnp.dot(centred, whitened.astype(jnp.float32).T, precision=highest)
            return value + jnp.dot(
                projected, white_innov.astype(jnp.float32), precision=highest
            ) / (members - 1)

        state = update(state)
        if b == 0:
            observed = update(pending).astype(jnp.bfloat16).astype(jnp.float32)
    return state


def solution(mesh):
    in_specs = (P(("row", "col"), None), P(), P(), P(), P(), P())
    out_specs = P(("row", "col"), None)
    return jax.shard_map(body, mesh=mesh, in_specs=in_specs, out_specs=out_specs, check_vma=False)
```

```python
import functools

import jax
import jax.numpy as jnp
from jax import lax
from jax.experimental import pallas as pl
from jax.experimental.pallas import tpu as pltpu
from jax.sharding import PartitionSpec as P

NX = 4
TILE_ROWS = 16
TILE_COLS = 128
MESH = pl.DeviceIdType.MESH


def split(value):
    high = value.astype(jnp.bfloat16)
    return high, (value - high.astype(jnp.float32)).astype(jnp.bfloat16)


def dot_tn(left, right):
    return lax.dot_general(
        left, right, (((0,), (0,)), ((), ())), preferred_element_type=jnp.float32
    )


def gather_kernel(nz, nx, ny, state_ref, blocks_ref, weights_ref, out_ref, *scratch):
    nb = blocks_ref.shape[0]
    batches = [scratch[7 * b : 7 * b + 7] for b in range(nb)]
    send_sems, recv_sems = scratch[7 * nb :]
    row = lax.axis_index("row")
    y = lax.axis_index("col")
    core = lax.rem(row, 2)
    x = lax.rem(row // 2, nx)
    z = row // (2 * nx)

    def place(z_, x_, core_, y_):
        return ((z_ * nx + x_) * 2 + core_, y_)

    core_peer = place(z, x, 1 - core, y)
    x_peers = [place(z, lax.rem(x + d, nx), core, y) for d in range(1, nx)]
    y_peers = [place(z, x, core, lax.rem(y + d, ny)) for d in range(1, ny)]
    z_peers = [place(lax.rem(z + d, nz), x, core, y) for d in range(1, nz)]
    peers = [core_peer, *x_peers, *y_peers, *z_peers]

    barrier = pltpu.get_barrier_semaphore()
    for peer in peers:
        pl.semaphore_signal(barrier, inc=1, device_id=peer, device_id_type=MESH)

    def interpolate(b):
        part = batches[b][0]
        rows = state_ref.shape[0]
        state_high, state_low = split(state_ref[...])
        observations = blocks_ref.shape[1]
        position = lax.broadcasted_iota(jnp.int32, (rows, observations), 0)
        first = (row * ny + y) * (rows // 4)
        held = blocks_ref[b : b + 1, :] - first == position // 4
        within = lax.rem(position, 4)
        weights = jnp.zeros((rows, observations), jnp.float32)
        for k in range(4):
            weights = jnp.where(within == k, weights_ref[b, k : k + 1, :], weights)
        selector_high, selector_low = split(jnp.where(held, weights, 0.0))
        values = (
            dot_tn(selector_low, state_high)
            + dot_tn(selector_high, state_low)
            + dot_tn(selector_high, state_high)
        ).astype(jnp.bfloat16)
        tile = 0
        per_x = part.shape[1] // nx
        half = part.shape[1]
        for i in range(values.shape[0] // TILE_ROWS):
            for j in range(values.shape[1] // TILE_COLS):
                part[tile // half, tile % half] = values[
                    i * TILE_ROWS : (i + 1) * TILE_ROWS, j * TILE_COLS : (j + 1) * TILE_COLS
                ]
                tile += 1

    def copy(b, index, source, target, peer):
        return pltpu.make_async_remote_copy(
            src_ref=source,
            dst_ref=target,
            send_sem=send_sems.at[b, index],
            recv_sem=recv_sems.at[b, index],
            device_id=peer,
            device_id_type=MESH,
        )

    per_x = batches[0][0].shape[1] // nx
    per_y = per_x // ny
    base = [0]
    for count in (1, nx - 1, ny - 1, nz - 1, ny - 1, nx - 1, 1):
        base.append(base[-1] + count)

    def start_stage(b, stage):
        part, from_core, from_x, from_y, from_z, mine, full = batches[b]
        copies = []
        if stage == 0:
            copies.append(copy(b, 0, part.at[1 - core], from_core, core_peer))
        elif stage == 1:
            for d in range(1, nx):
                target = lax.rem(x + d, nx)
                source = part.at[core, pl.ds(target * per_x, per_x)]
                copies.append(copy(b, base[1] + d - 1, source, from_x.at[d - 1], x_peers[d - 1]))
        elif stage == 2:
            for d in range(1, ny):
                target = lax.rem(y + d, ny)
                source = part.at[core, pl.ds(x * per_x + target * per_y, per_y)]
                copies.append(copy(b, base[2] + d - 1, source, from_y.at[d - 1], y_peers[d - 1]))
        elif stage == 3:
            for d in range(1, nz):
                copies.append(copy(b, base[3] + d - 1, mine, from_z.at[d - 1], z_peers[d - 1]))
        elif stage == 4:
            whole = full.at[core, x, y]
            for d in range(1, ny):
                copies.append(copy(b, base[4] + d - 1, whole, whole, y_peers[d - 1]))
        elif stage == 5:
            whole = full.at[core, x]
            for d in range(1, nx):
                copies.append(copy(b, base[5] + d - 1, whole, whole, x_peers[d - 1]))
        else:
            whole = full.at[core]
            copies.append(copy(b, base[6], whole, whole, core_peer))
        for each in copies:
            each.start()
        return copies

    def finish_stage(b, stage, copies):
        part, from_core, from_x, from_y, from_z, mine, full = batches[b]
        for each in copies:
            each.wait_recv()
        if stage == 0:
            part[core] = part[core] + from_core[...]
        elif stage == 1:
            here = pl.ds(x * per_x, per_x)
            part[core, here] = part[core, here] + functools.reduce(
                jnp.add, [from_x[d] for d in range(nx - 1)]
            )
        elif stage == 2:
            here = pl.ds(x * per_x + y * per_y, per_y)
            mine[...] = part[core, here] + functools.reduce(
                jnp.add, [from_y[d] for d in range(ny - 1)]
            )
        elif stage == 3:
            full[core, x, y] = mine[...] + functools.reduce(
                jnp.add, [from_z[d] for d in range(nz - 1)]
            )

    started = [[] for _ in range(nb)]
    current = [None] * nb
    for b in range(nb):
        interpolate(b)
        if b == 0:
            pl.semaphore_wait(barrier, len(peers))
        current[b] = start_stage(b, 0)
        started[b] += current[b]
    for stage in range(7):
        for b in range(nb):
            finish_stage(b, stage, current[b])
            if stage < 6:
                current[b] = start_stage(b, stage + 1)
                started[b] += current[b]
    for b in range(nb):
        full = batches[b][6]
        columns = out_ref.shape[2] // TILE_COLS
        for i in range(out_ref.shape[1] // TILE_ROWS):
            for j in range(columns):
                tile = i * columns + j
                c, rest = divmod(tile, nx * per_x)
                x_, rest = divmod(rest, per_x)
                y_, t = divmod(rest, per_y)
                out_ref[
                    b, i * TILE_ROWS : (i + 1) * TILE_ROWS, j * TILE_COLS : (j + 1) * TILE_COLS
                ] = full[c, x_, y_, t]
    for b in range(nb):
        for each in started[b]:
            each.wait_send()


def gather_observed(ensemble, obs_blocks, obs_weights):
    nx = NX
    ny = lax.axis_size("col")
    nz = lax.axis_size("row") // (2 * nx)
    batches, observations = obs_blocks.shape
    members = ensemble.shape[1]
    tiles = observations * members // (TILE_ROWS * TILE_COLS)
    per_x = tiles // (2 * nx)
    per_y = per_x // ny
    tile = (TILE_ROWS, TILE_COLS)
    one_batch = [
        pltpu.VMEM((2, tiles // 2, *tile), jnp.bfloat16),
        pltpu.VMEM((tiles // 2, *tile), jnp.bfloat16),
        pltpu.VMEM((nx - 1, per_x, *tile), jnp.bfloat16),
        pltpu.VMEM((ny - 1, per_y, *tile), jnp.bfloat16),
        pltpu.VMEM((nz - 1, per_y, *tile), jnp.bfloat16),
        pltpu.VMEM((per_y, *tile), jnp.bfloat16),
        pltpu.VMEM((2, nx, ny, per_y, *tile), jnp.bfloat16),
    ]
    copies = 2 * (1 + nx - 1 + ny - 1) + nz - 1
    vmem = pl.BlockSpec(memory_space=pltpu.VMEM)
    return pl.pallas_call(
        functools.partial(gather_kernel, nz, nx, ny),
        out_shape=jax.ShapeDtypeStruct((batches, observations, members), jnp.bfloat16),
        in_specs=[vmem] * 3,
        out_specs=vmem,
        scratch_shapes=one_batch * batches
        + [
            pltpu.SemaphoreType.DMA((batches, copies)),
            pltpu.SemaphoreType.DMA((batches, copies)),
        ],
        compiler_params=pltpu.CompilerParams(
            collective_id=0, has_side_effects=True, vmem_limit_bytes=32 * 1024 * 1024
        ),
        cost_estimate=pl.CostEstimate(flops=10**8, bytes_accessed=10**7, transcendentals=0),
        name="gather_observed",
    )(ensemble, obs_blocks, jnp.transpose(obs_weights, (0, 2, 1)))


PANEL, SUB = 32, 16

def parts_of(value, count):
    parts = []
    for _ in range(count):
        part = value.astype(jnp.bfloat16)
        parts.append(part)
        value = value - part.astype(jnp.float32)
    return parts

def factor_inverse(m_ref, t_ref):
    panel, sub = PANEL, SUB
    size = m_ref.shape[0]
    lanes = lax.broadcasted_iota(jnp.int32, (panel, 128), 1)
    rows_of = lax.broadcasted_iota(jnp.int32, (panel, 128), 0)
    rows8 = lax.broadcasted_iota(jnp.int32, (8, 128), 0)
    for start in range(0, size, panel):
        tile, lane0 = start // 128, start % 128
        here = pl.ds(start, panel)
        block = m_ref[here, tile * 128 : tile * 128 + 128]
        wide = []
        for t in range(size // 128):
            part = block if t == tile else m_ref[here, t * 128 : t * 128 + 128]
            if t == tile:
                inside = (lanes >= lane0) & (lanes < lane0 + panel)
                part = jnp.where(inside, jnp.where(lanes - lane0 == rows_of, 1.0, 0.0), part)
            wide.append(part)
        wide.append(block)
        done = [[] for _ in wide]
        scales = []
        top = 0
        for s in range(0, panel, sub):
            columns = {
                j: jnp.broadcast_to(wide[-1][:, lane0 + j : lane0 + j + 1], wide[-1].shape)
                for j in range(s, s + sub)
            }
            for k in range(s, s + sub):
                if k - top == 8:
                    for i, part in enumerate(wide):
                        done[i].append(part[:8])
                        wide[i] = part[8:]
                    columns = {j: c[8:] for j, c in columns.items() if j >= k}
                    top += 8
                at = k - top
                if at == 0:
                    scale = jnp.zeros((8, 128), jnp.float32)
                pivot = columns[k][at : at + 1]
                inverse = 1.0 / pivot
                scale = jnp.where(rows8 == at, lax.rsqrt(pivot), scale)
                below = rows_of[: panel - top] > at
                multiple = jnp.where(below, columns[k] * inverse, 0.0)
                for j in range(k + 1, s + sub):
                    columns[j] = columns[j] - multiple * columns[j][at : at + 1]
                last = len(wide) if s + sub < panel else len(wide) - 1
                for i in range(last):
                    wide[i] = wide[i] - multiple * wide[i][at : at + 1]
                if at == 7:
                    scales.append(scale)
        for i, part in enumerate(wide):
            done[i].append(part)
        scale = jnp.concatenate(scales, axis=0)
        scaled = [jnp.concatenate(done[i], axis=0) * scale for i in range(size // 128)]
        for t in range(size // 128):
            kept = scaled[t]
            if t == tile:
                kept = jnp.where(lanes < lane0 + panel, kept, 0.0)
            elif t > tile:
                kept = jnp.zeros_like(kept)
            t_ref[here, t * 128 : t * 128 + 128] = kept
        after = start + panel
        if after < size:
            first = after // 128
            whole = jnp.concatenate(scaled, axis=1)
            p = parts_of(whole, 3)
            left = [p[0], p[0], p[1], p[1], p[0], p[2]]
            right = [p[0], p[1], p[0], p[1], p[2], p[0]]
            left = jnp.concatenate(left, axis=0)[:, first * 128 :]
            right = jnp.concatenate(right, axis=0)
            product = lax.dot_general(
                left, right, (((0,), (0,)), ((), ())), preferred_element_type=jnp.float32
            )[after - first * 128 :]
            for t in range(size // 128):
                old = m_ref[after:, t * 128 : t * 128 + 128]
                if t == tile:
                    at_lane = lax.broadcasted_iota(jnp.int32, old.shape, 1)
                    old = jnp.where((at_lane >= lane0) & (at_lane < lane0 + panel), 0.0, old)
                m_ref[after:, t * 128 : t * 128 + 128] = old - product[:, t * 128 : t * 128 + 128]


def dot_nt(left, right):
    return lax.dot_general(
        left, right, (((1,), (1,)), ((), ())), preferred_element_type=jnp.float32
    )


def three_pass(dot, left, right):
    (left_high, left_low), (right_high, right_low) = left, right
    return dot(left_high, right_low) + dot(left_low, right_high) + dot(left_high, right_high)


def dot_nn(left, right):
    return jnp.dot(left, right, preferred_element_type=jnp.float32)


def analysis_kernel(
    raw_ref, state_ref, noise_ref, tags_ref, values_ref, out_ref, rows_ref, m_ref, t_ref
):
    local_rows, members = state_ref.shape
    batches, observations = tags_ref.shape
    variances = jnp.where(tags_ref[...] == 0, jnp.float32(0.5), jnp.float32(2.0))
    fill = jnp.zeros((8 - 2 * batches, observations), jnp.float32)
    by_row = jnp.concatenate([values_ref[...], jnp.sqrt(variances), fill], axis=0).T
    shape = (observations, observations)
    diagonal = lax.broadcasted_iota(jnp.int32, shape, 0) == lax.broadcasted_iota(
        jnp.int32, shape, 1
    )
    rows_ref[:local_rows] = state_ref[...]
    rows_ref[local_rows:] = raw_ref[1].astype(jnp.float32)
    for b in range(batches):
        if b == 0:
            observed = raw_ref[0].astype(jnp.float32)
        else:
            observed = rows_ref[local_rows:].astype(jnp.bfloat16).astype(jnp.float32)
        anomalies = split(observed - jnp.mean(observed, axis=1, keepdims=True))
        covariance = three_pass(dot_nt, anomalies, anomalies) * (1.0 / (members - 1))
        m_ref[...] = covariance + jnp.where(diagonal, variances[b : b + 1], 0.0)
        count = rows_ref.shape[0] if b + 1 < batches else local_rows
        rows = rows_ref[:count]
        centred = split(rows - jnp.mean(rows, axis=1, keepdims=True))
        product = split(three_pass(dot_nt, centred, anomalies) * (1.0 / (members - 1)))
        innovation = split(
            by_row[:, b : b + 1]
            + by_row[:, batches + b : batches + b + 1] * noise_ref[b].astype(jnp.float32)
            - observed
        )
        factor_inverse(m_ref, t_ref)
        inverse = split(t_ref[...])
        projected_high, projected_low = split(three_pass(dot_nt, product, inverse))
        white_innov = three_pass(dot_nn, inverse, innovation).astype(jnp.bfloat16)
        change = dot_nn(projected_low, white_innov) + dot_nn(projected_high, white_innov)
        if b + 1 < batches:
            rows_ref[:count] = rows + change
        else:
            out_ref[...] = rows + change


def analyse(raw, ensemble, obs_noise, comp_tags, obs_values):
    local_rows, members = ensemble.shape
    observations = comp_tags.shape[1]
    vmem = pl.BlockSpec(memory_space=pltpu.VMEM)
    square = pltpu.VMEM((observations, observations), jnp.float32)
    return pl.pallas_call(
        analysis_kernel,
        out_shape=jax.ShapeDtypeStruct(ensemble.shape, jnp.float32),
        in_specs=[vmem] * 5,
        out_specs=vmem,
        scratch_shapes=[
            pltpu.VMEM((local_rows + observations, members), jnp.float32),
            square,
            square,
        ],
        compiler_params=pltpu.CompilerParams(vmem_limit_bytes=48 * 1024 * 1024),
        cost_estimate=pl.CostEstimate(flops=10**10, bytes_accessed=10**7, transcendentals=0),
        name="analyse",
    )(raw, ensemble, obs_noise, comp_tags, obs_values)


def body(ensemble, obs_blocks, obs_weights, comp_tags, obs_values, obs_noise):
    raw = gather_observed(ensemble, obs_blocks, obs_weights)
    return analyse(raw, ensemble, obs_noise, comp_tags, obs_values)


def solution(mesh):
    in_specs = (P(("row", "col"), None), P(), P(), P(), P(), P())
    out_specs = P(("row", "col"), None)
    return jax.shard_map(body, mesh=mesh, in_specs=in_specs, out_specs=out_specs, check_vma=False)
```

```python
import functools

import jax
import jax.numpy as jnp
from jax import lax
from jax.experimental import pallas as pl
from jax.experimental.pallas import tpu as pltpu
from jax.sharding import PartitionSpec as P

NX = 4
PIECES = 4
TILE_ROWS = 16
TILE_COLS = 128
MESH = pl.DeviceIdType.MESH


def farthest_first(count):
    return sorted(range(1, count), key=lambda d: -min(d, count - d))


def split(value):
    high = value.astype(jnp.bfloat16)
    return high, (value - high.astype(jnp.float32)).astype(jnp.bfloat16)


def dot_tn(left, right):
    return lax.dot_general(
        left, right, (((0,), (0,)), ((), ())), preferred_element_type=jnp.float32
    )


def filter_kernel(nz, nx, ny, *refs):
    hbm, out_ref, local = refs[:6], refs[6], refs[7:13]
    rows_ref, raw_ref, m_ref, t_ref, load_sems, send_sems, recv_sems = refs[13:20]
    y_relay, z_relay, scratch = refs[20:22], refs[22:25], refs[25:]
    state_ref, blocks_ref, weights_ref, tags_ref, values_ref, noise_ref = local
    nb = blocks_ref.shape[0]
    batches = [scratch[7 * b : 7 * b + 7] for b in range(nb)]
    piece = state_ref.shape[0] // PIECES
    pairs = [
        (hbm[0].at[pl.ds(i * piece, piece)], state_ref.at[pl.ds(i * piece, piece)])
        for i in range(PIECES)
    ]
    pairs = [*zip(hbm[1:3], local[1:3]), *pairs, *zip(hbm[3:], local[3:])]
    loads = [
        pltpu.make_async_copy(source, target, load_sems.at[i])
        for i, (source, target) in enumerate(pairs)
    ]
    early, late = loads[: 2 + PIECES], loads[2 + PIECES :]
    for load in early:
        load.start()
    row = lax.axis_index("row")
    y = lax.axis_index("col")
    core = lax.rem(row, 2)
    x = lax.rem(row // 2, nx)
    z = row // (2 * nx)

    def place(z_, x_, core_, y_):
        return ((z_ * nx + x_) * 2 + core_, y_)

    core_peer = place(z, x, 1 - core, y)
    x_peers = [place(z, lax.rem(x + d, nx), core, y) for d in range(1, nx)]
    y_peers = [place(z, x, core, lax.rem(y + d, ny)) for d in range(1, ny)]
    z_peers = [place(lax.rem(z + d, nz), x, core, y) for d in range(1, nz)]

    def ring(peers, distance):
        return (peers[distance - 1], peers[-distance])

    peers = [core_peer, *x_peers, *ring(y_peers, 1), *ring(z_peers, 1)]

    def tell(sem, targets):
        for target in targets:
            pl.semaphore_signal(sem, inc=1, device_id=target, device_id_type=MESH)

    def meet_y():
        pl.semaphore_wait(y_relay[0], 2)
        tell(y_relay[1], ring(y_peers, 2))

    def meet_z(step):
        pl.semaphore_wait(z_relay[step], 2)
        tell(z_relay[step + 1], ring(z_peers, 2))

    barrier = pltpu.get_barrier_semaphore()
    for peer in peers:
        pl.semaphore_signal(barrier, inc=1, device_id=peer, device_id_type=MESH)

    def interpolate(b):
        part = batches[b][0]
        rows = state_ref.shape[0]
        state_high, state_low = split(state_ref[...])
        observations = blocks_ref.shape[1]
        position = lax.broadcasted_iota(jnp.int32, (rows, observations), 0)
        first = (row * ny + y) * (rows // 4)
        held = blocks_ref[b : b + 1, :] - first == position // 4
        within = lax.rem(position, 4)
        weights = jnp.zeros((rows, observations), jnp.float32)
        for k in range(4):
            weights = jnp.where(within == k, weights_ref[b, k : k + 1, :], weights)
        selector_high, selector_low = split(jnp.where(held, weights, 0.0))
        values = (
            dot_tn(selector_low, state_high)
            + dot_tn(selector_high, state_low)
            + dot_tn(selector_high, state_high)
        ).astype(jnp.bfloat16)
        tile = 0
        per_x = part.shape[1] // nx
        half = part.shape[1]
        for i in range(values.shape[0] // TILE_ROWS):
            for j in range(values.shape[1] // TILE_COLS):
                part[tile // half, tile % half] = values[
                    i * TILE_ROWS : (i + 1) * TILE_ROWS, j * TILE_COLS : (j + 1) * TILE_COLS
                ]
                tile += 1

    def copy(b, index, source, target, peer):
        return pltpu.make_async_remote_copy(
            src_ref=source,
            dst_ref=target,
            send_sem=send_sems.at[b, index],
            recv_sem=recv_sems.at[b, index],
            device_id=peer,
            device_id_type=MESH,
        )

    per_x = batches[0][0].shape[1] // nx
    per_y = per_x // ny
    base = [0]
    for count in (1, nx - 1, ny - 1, nz - 1, ny - 1, nx - 1, 1):
        base.append(base[-1] + count)

    def start_stage(b, stage):
        part, from_core, from_x, from_y, from_z, mine, full = batches[b]
        copies = []
        if stage == 0:
            copies.append(copy(b, 0, part.at[1 - core], from_core, core_peer))
        elif stage == 1:
            for d in farthest_first(nx):
                target = lax.rem(x + d, nx)
                source = part.at[core, pl.ds(target * per_x, per_x)]
                copies.append(copy(b, base[1] + d - 1, source, from_x.at[d - 1], x_peers[d - 1]))
        elif stage == 2:
            for d in farthest_first(ny):
                target = lax.rem(y + d, ny)
                source = part.at[core, pl.ds(x * per_x + target * per_y, per_y)]
                copies.append(copy(b, base[2] + d - 1, source, from_y.at[d - 1], y_peers[d - 1]))
        elif stage == 3:
            for d in farthest_first(nz):
                copies.append(copy(b, base[3] + d - 1, mine, from_z.at[d - 1], z_peers[d - 1]))
        elif stage == 4:
            whole = full.at[core, x, y]
            for d in farthest_first(ny):
                copies.append(copy(b, base[4] + d - 1, whole, whole, y_peers[d - 1]))
        elif stage == 5:
            whole = full.at[core, x]
            for d in farthest_first(nx):
                copies.append(copy(b, base[5] + d - 1, whole, whole, x_peers[d - 1]))
        else:
            whole = full.at[core]
            copies.append(copy(b, base[6], whole, whole, core_peer))
        for each in copies:
            each.start()
        return copies

    def finish_stage(b, stage, copies):
        part, from_core, from_x, from_y, from_z, mine, full = batches[b]
        for each in copies:
            each.wait_recv()
        if stage == 0:
            part[core] = part[core] + from_core[...]
        elif stage == 1:
            here = pl.ds(x * per_x, per_x)
            part[core, here] = part[core, here] + functools.reduce(
                jnp.add, [from_x[d] for d in range(nx - 1)]
            )
        elif stage == 2:
            here = pl.ds(x * per_x + y * per_y, per_y)
            mine[...] = part[core, here] + functools.reduce(
                jnp.add, [from_y[d] for d in range(ny - 1)]
            )
        elif stage == 3:
            full[core, x, y] = mine[...] + functools.reduce(
                jnp.add, [from_z[d] for d in range(nz - 1)]
            )

    started = [[] for _ in range(nb)]
    current = [None] * nb

    def begin(b, stage):
        current[b] = start_stage(b, stage)
        started[b] += current[b]

    def advance(b, stage):
        finish_stage(b, stage, current[b])
        if stage < 6:
            begin(b, stage + 1)

    def assemble(b):
        full = batches[b][6]
        columns = raw_ref.shape[2] // TILE_COLS
        for i in range(raw_ref.shape[1] // TILE_ROWS):
            for j in range(columns):
                tile = i * columns + j
                c, rest = divmod(tile, nx * per_x)
                x_, rest = divmod(rest, per_x)
                y_, t = divmod(rest, per_y)
                raw_ref[
                    b, i * TILE_ROWS : (i + 1) * TILE_ROWS, j * TILE_COLS : (j + 1) * TILE_COLS
                ] = full[c, x_, y_, t]

    for load in early:
        load.wait()
    for load in late:
        load.start()
    interpolate(0)
    pl.semaphore_wait(barrier, len(peers))
    tell(y_relay[0], ring(y_peers, 1))
    tell(z_relay[0], ring(z_peers, 1))
    begin(0, 0)
    interpolate(1)
    advance(0, 0)
    begin(1, 0)
    meet_y()
    meet_z(0)
    advance(1, 0)
    pl.semaphore_wait(y_relay[1], 2)
    advance(0, 1)
    meet_z(1)
    advance(1, 1)
    pl.semaphore_wait(z_relay[2], 2)
    for stage in range(2, 5):
        advance(0, stage)
        advance(1, stage)
    advance(0, 5)
    advance(0, 6)
    assemble(0)
    for load in late:
        load.wait()

    def receive():
        advance(1, 5)

    def receive_last():
        advance(1, 6)
        assemble(1)

    analyse(
        raw_ref,
        state_ref,
        noise_ref,
        tags_ref,
        values_ref,
        out_ref,
        rows_ref,
        m_ref,
        t_ref,
        receive,
        receive_last,
    )
    for b in range(nb):
        for each in started[b]:
            each.wait_send()


def filter_call(ensemble, obs_blocks, obs_weights, comp_tags, obs_values, obs_noise):
    nx = NX
    ny = lax.axis_size("col")
    nz = lax.axis_size("row") // (2 * nx)
    batches, observations = obs_blocks.shape
    members = ensemble.shape[1]
    tiles = observations * members // (TILE_ROWS * TILE_COLS)
    per_x = tiles // (2 * nx)
    per_y = per_x // ny
    tile = (TILE_ROWS, TILE_COLS)
    one_batch = [
        pltpu.VMEM((2, tiles // 2, *tile), jnp.bfloat16),
        pltpu.VMEM((tiles // 2, *tile), jnp.bfloat16),
        pltpu.VMEM((nx - 1, per_x, *tile), jnp.bfloat16),
        pltpu.VMEM((ny - 1, per_y, *tile), jnp.bfloat16),
        pltpu.VMEM((nz - 1, per_y, *tile), jnp.bfloat16),
        pltpu.VMEM((per_y, *tile), jnp.bfloat16),
        pltpu.VMEM((2, nx, ny, per_y, *tile), jnp.bfloat16),
    ]
    copies = 2 * (1 + nx - 1 + ny - 1) + nz - 1
    weights = jnp.transpose(obs_weights, (0, 2, 1))
    operands = (ensemble, obs_blocks, weights, comp_tags, obs_values, obs_noise)
    square = pltpu.VMEM((observations, observations), jnp.float32)
    return pl.pallas_call(
        functools.partial(filter_kernel, nz, nx, ny),
        out_shape=jax.ShapeDtypeStruct(ensemble.shape, jnp.float32),
        in_specs=[pl.BlockSpec(memory_space=pltpu.HBM)] * len(operands),
        out_specs=pl.BlockSpec(memory_space=pltpu.VMEM),
        scratch_shapes=[pltpu.VMEM(value.shape, value.dtype) for value in operands]
        + [
            pltpu.VMEM((observations, members), jnp.float32),
            pltpu.VMEM((batches, observations, members), jnp.bfloat16),
            square,
            square,
            pltpu.SemaphoreType.DMA((len(operands) - 1 + PIECES,)),
            pltpu.SemaphoreType.DMA((batches, copies)),
            pltpu.SemaphoreType.DMA((batches, copies)),
        ]
        + [pltpu.SemaphoreType.REGULAR] * 5
        + one_batch * batches,
        compiler_params=pltpu.CompilerParams(
            collective_id=0, has_side_effects=True, vmem_limit_bytes=60 * 1024 * 1024
        ),
        cost_estimate=pl.CostEstimate(flops=10**10, bytes_accessed=10**7, transcendentals=0),
        name="ensemble_filter",
    )(*operands)


PANEL, SUB = 32, 16

def parts_of(value, count):
    parts = []
    for _ in range(count):
        part = value.astype(jnp.bfloat16)
        parts.append(part)
        value = value - part.astype(jnp.float32)
    return parts

def factor_inverse(m_ref, t_ref, meanwhile):
    panel, sub = PANEL, SUB
    size = m_ref.shape[0]
    lanes = lax.broadcasted_iota(jnp.int32, (panel, 128), 1)
    rows_of = lax.broadcasted_iota(jnp.int32, (panel, 128), 0)
    rows8 = lax.broadcasted_iota(jnp.int32, (8, 128), 0)
    for start in range(0, size, panel):
        tile, lane0 = start // 128, start % 128
        here = pl.ds(start, panel)
        block = m_ref[here, tile * 128 : tile * 128 + 128]
        wide = []
        for t in range(size // 128):
            part = block if t == tile else m_ref[here, t * 128 : t * 128 + 128]
            if t == tile:
                inside = (lanes >= lane0) & (lanes < lane0 + panel)
                part = jnp.where(inside, jnp.where(lanes - lane0 == rows_of, 1.0, 0.0), part)
            wide.append(part)
        wide.append(block)
        done = [[] for _ in wide]
        scales = []
        top = 0
        for s in range(0, panel, sub):
            columns = {
                j: jnp.broadcast_to(wide[-1][:, lane0 + j : lane0 + j + 1], wide[-1].shape)
                for j in range(s, s + sub)
            }
            for k in range(s, s + sub):
                if k - top == 8:
                    for i, part in enumerate(wide):
                        done[i].append(part[:8])
                        wide[i] = part[8:]
                    columns = {j: c[8:] for j, c in columns.items() if j >= k}
                    top += 8
                at = k - top
                if at == 0:
                    scale = jnp.zeros((8, 128), jnp.float32)
                pivot = columns[k][at : at + 1]
                inverse = 1.0 / pivot
                scale = jnp.where(rows8 == at, lax.rsqrt(pivot), scale)
                below = rows_of[: panel - top] > at
                multiple = jnp.where(below, columns[k] * inverse, 0.0)
                for j in range(k + 1, s + sub):
                    columns[j] = columns[j] - multiple * columns[j][at : at + 1]
                last = len(wide) if s + sub < panel else len(wide) - 1
                for i in range(last):
                    wide[i] = wide[i] - multiple * wide[i][at : at + 1]
                if at == 7:
                    scales.append(scale)
        for i, part in enumerate(wide):
            done[i].append(part)
        scale = jnp.concatenate(scales, axis=0)
        scaled = [jnp.concatenate(done[i], axis=0) * scale for i in range(size // 128)]
        for t in range(size // 128):
            kept = scaled[t]
            if t == tile:
                kept = jnp.where(lanes < lane0 + panel, kept, 0.0)
            elif t > tile:
                kept = jnp.zeros_like(kept)
            t_ref[here, t * 128 : t * 128 + 128] = kept
        after = start + panel
        if after < size:
            first = after // 128
            whole = jnp.concatenate(scaled, axis=1)
            p = parts_of(whole, 3)
            left = [p[0], p[0], p[1], p[1], p[0], p[2]]
            right = [p[0], p[1], p[0], p[1], p[2], p[0]]
            left = jnp.concatenate(left, axis=0)[:, first * 128 :]
            right = jnp.concatenate(right, axis=0)
            product = lax.dot_general(
                left, right, (((0,), (0,)), ((), ())), preferred_element_type=jnp.float32
            )[after - first * 128 :]
            for t in range(size // 128):
                old = m_ref[after:, t * 128 : t * 128 + 128]
                if t == tile:
                    at_lane = lax.broadcasted_iota(jnp.int32, old.shape, 1)
                    old = jnp.where((at_lane >= lane0) & (at_lane < lane0 + panel), 0.0, old)
                m_ref[after:, t * 128 : t * 128 + 128] = old - product[:, t * 128 : t * 128 + 128]
            meanwhile(start // panel)


def dot_nt(left, right):
    return lax.dot_general(
        left, right, (((1,), (1,)), ((), ())), preferred_element_type=jnp.float32
    )


def three_pass(dot, left, right):
    (left_high, left_low), (right_high, right_low) = left, right
    return dot(left_high, right_low) + dot(left_low, right_high) + dot(left_high, right_high)


def dot_nn(left, right):
    return jnp.dot(left, right, preferred_element_type=jnp.float32)


def centre(value):
    return split(value - jnp.mean(value, axis=1, keepdims=True))


def analyse(
    raw_ref,
    state_ref,
    noise_ref,
    tags_ref,
    values_ref,
    out_ref,
    pending_ref,
    m_ref,
    t_ref,
    receive,
    receive_last,
):
    members = state_ref.shape[1]
    batches, observations = tags_ref.shape
    half = observations // 2
    share = 1.0 / (members - 1)
    variances = jnp.where(tags_ref[...] == 0, jnp.float32(0.5), jnp.float32(2.0))
    fill = jnp.zeros((8 - 2 * batches, observations), jnp.float32)
    by_row = jnp.concatenate([values_ref[...], jnp.sqrt(variances), fill], axis=0).T
    shape = (observations, observations)
    diagonal = lax.broadcasted_iota(jnp.int32, shape, 0) == lax.broadcasted_iota(
        jnp.int32, shape, 1
    )

    def project(value, anomalies):
        return split(three_pass(dot_nt, centre(value), anomalies) * share)

    def columns(pair, start, stop):
        return tuple(part[:, start:stop] for part in pair)

    def rows(pair, start, stop):
        return tuple(part[start:stop] for part in pair)

    def change(projected, white_innov):
        high, low = projected
        return dot_nn(low, white_innov) + dot_nn(high, white_innov)

    found = {}
    for b in range(batches):
        if b == 0:
            observed = raw_ref[0].astype(jnp.float32)
        else:
            observed = pending_ref[...].astype(jnp.bfloat16).astype(jnp.float32)
        anomalies = centre(observed)
        covariance = three_pass(dot_nt, anomalies, anomalies) * share
        m_ref[...] = covariance + jnp.where(diagonal, variances[b : b + 1], 0.0)

        def meanwhile(panel, b=b, observed=observed, anomalies=anomalies):
            if panel == 0:
                if b:
                    state_ref[...] += change(*found["change"])
                noise = noise_ref[b].astype(jnp.float32)
                scale = by_row[:, batches + b : batches + b + 1]
                found["innovation"] = split(by_row[:, b : b + 1] + scale * noise - observed)
            elif panel == 1:
                found["state"] = project(state_ref[...], anomalies)
                if b == 0:
                    receive()
            elif panel == 3:
                inverse = split(t_ref[:half, :half])
                top = rows(found["innovation"], 0, half)
                found["white"] = three_pass(dot_nn, inverse, top).astype(jnp.bfloat16)
                found["top"] = inverse
            elif panel == 4:
                found["left"] = three_pass(
                    dot_nt, columns(found["state"], 0, half), found["top"]
                )
                if b == 0:
                    receive_last()
                    found["pending"] = project(raw_ref[1].astype(jnp.float32), anomalies)
            elif panel == 5 and b == 0:
                found["pending_left"] = three_pass(
                    dot_nt, columns(found["pending"], 0, half), found["top"]
                )

        factor_inverse(m_ref, t_ref, meanwhile)
        inverse = split(t_ref[half:])
        bottom = three_pass(dot_nn, inverse, found["innovation"]).astype(jnp.bfloat16)
        white_innov = jnp.concatenate([found["white"], bottom], axis=0)

        def projected(left, product):
            right = three_pass(dot_nt, product, inverse)
            return split(jnp.concatenate([left, right], axis=1))

        if b + 1 < batches:
            pending = projected(found["pending_left"], found["pending"])
            pending_ref[...] = raw_ref[1].astype(jnp.float32) + change(pending, white_innov)
            found["change"] = (projected(found["left"], found["state"]), white_innov)
        else:
            out_ref[...] = state_ref[...] + change(
                projected(found["left"], found["state"]), white_innov
            )


def solution(mesh):
    in_specs = (P(("row", "col"), None), P(), P(), P(), P(), P())
    out_specs = P(("row", "col"), None)
    return jax.shard_map(filter_call, mesh=mesh, in_specs=in_specs, out_specs=out_specs, check_vma=False)
```

```python
import functools

import jax
import jax.numpy as jnp
from jax import lax
from jax.experimental import pallas as pl
from jax.experimental.pallas import tpu as pltpu
from jax.sharding import PartitionSpec as P

NX = 4
PIECES = 4
TILE_ROWS = 16
TILE_COLS = 128
MESH = pl.DeviceIdType.MESH


def farthest_first(count):
    return sorted(range(1, count), key=lambda d: -min(d, count - d))


def split(value):
    high = value.astype(jnp.bfloat16)
    return high, (value - high.astype(jnp.float32)).astype(jnp.bfloat16)


def dot_tn(left, right):
    return lax.dot_general(
        left, right, (((0,), (0,)), ((), ())), preferred_element_type=jnp.float32
    )


def filter_kernel(nz, nx, ny, *refs):
    hbm, out_hbm, local = refs[:6], refs[6], refs[7:13]
    rows_ref, raw_ref, m_ref, t_ref, out_ref, load_sems, send_sems, recv_sems = refs[13:21]
    y_relay, z_relay, scratch = refs[21:23], refs[23:26], refs[26:]
    state_ref, blocks_ref, weights_ref, tags_ref, values_ref, noise_ref = local
    nb = blocks_ref.shape[0]
    batches = [scratch[7 * b : 7 * b + 7] for b in range(nb)]
    piece = state_ref.shape[0] // PIECES
    pairs = [
        (hbm[0].at[pl.ds(i * piece, piece)], state_ref.at[pl.ds(i * piece, piece)])
        for i in range(PIECES)
    ]
    pairs = [*zip(hbm[1:3], local[1:3]), *pairs, *zip(hbm[3:], local[3:])]
    loads = [
        pltpu.make_async_copy(source, target, load_sems.at[i])
        for i, (source, target) in enumerate(pairs)
    ]
    early, late = loads[: 2 + PIECES], loads[2 + PIECES :]
    for load in early:
        load.start()
    row = lax.axis_index("row")
    y = lax.axis_index("col")
    core = lax.rem(row, 2)
    x = lax.rem(row // 2, nx)
    z = row // (2 * nx)

    def place(z_, x_, core_, y_):
        return ((z_ * nx + x_) * 2 + core_, y_)

    core_peer = place(z, x, 1 - core, y)
    x_peers = [place(z, lax.rem(x + d, nx), core, y) for d in range(1, nx)]
    y_peers = [place(z, x, core, lax.rem(y + d, ny)) for d in range(1, ny)]
    z_peers = [place(lax.rem(z + d, nz), x, core, y) for d in range(1, nz)]

    def ring(peers, distance):
        return (peers[distance - 1], peers[-distance])

    peers = [core_peer, *x_peers, *ring(y_peers, 1), *ring(z_peers, 1)]

    def tell(sem, targets):
        for target in targets:
            pl.semaphore_signal(sem, inc=1, device_id=target, device_id_type=MESH)

    def meet_y():
        pl.semaphore_wait(y_relay[0], 2)
        tell(y_relay[1], ring(y_peers, 2))

    def meet_z(step):
        pl.semaphore_wait(z_relay[step], 2)
        tell(z_relay[step + 1], ring(z_peers, 2))

    barrier = pltpu.get_barrier_semaphore()
    for peer in peers:
        pl.semaphore_signal(barrier, inc=1, device_id=peer, device_id_type=MESH)

    def interpolate(b):
        part = batches[b][0]
        rows = state_ref.shape[0]
        state_high, state_low = split(state_ref[...])
        observations = blocks_ref.shape[1]
        position = lax.broadcasted_iota(jnp.int32, (rows, observations), 0)
        first = (row * ny + y) * (rows // 4)
        held = blocks_ref[b : b + 1, :] - first == position // 4
        within = lax.rem(position, 4)
        weights = jnp.zeros((rows, observations), jnp.float32)
        for k in range(4):
            weights = jnp.where(within == k, weights_ref[b, k : k + 1, :], weights)
        selector_high, selector_low = split(jnp.where(held, weights, 0.0))
        values = (
            dot_tn(selector_low, state_high)
            + dot_tn(selector_high, state_low)
            + dot_tn(selector_high, state_high)
        ).astype(jnp.bfloat16)
        tile = 0
        per_x = part.shape[1] // nx
        half = part.shape[1]
        for i in range(values.shape[0] // TILE_ROWS):
            for j in range(values.shape[1] // TILE_COLS):
                part[tile // half, tile % half] = values[
                    i * TILE_ROWS : (i + 1) * TILE_ROWS, j * TILE_COLS : (j + 1) * TILE_COLS
                ]
                tile += 1

    def copy(b, index, source, target, peer):
        return pltpu.make_async_remote_copy(
            src_ref=source,
            dst_ref=target,
            send_sem=send_sems.at[b, index],
            recv_sem=recv_sems.at[b, index],
            device_id=peer,
            device_id_type=MESH,
        )

    per_x = batches[0][0].shape[1] // nx
    per_y = per_x // ny
    base = [0]
    for count in (1, nx - 1, ny - 1, nz - 1, ny - 1, nx - 1, nx):
        base.append(base[-1] + count)

    def start_stage(b, stage):
        part, from_core, from_x, from_y, from_z, mine, full = batches[b]
        copies = []
        if stage == 0:
            copies.append(copy(b, 0, part.at[1 - core], from_core, core_peer))
        elif stage == 1:
            for d in farthest_first(nx):
                target = lax.rem(x + d, nx)
                source = part.at[core, pl.ds(target * per_x, per_x)]
                copies.append(copy(b, base[1] + d - 1, source, from_x.at[d - 1], x_peers[d - 1]))
        elif stage == 2:
            for d in farthest_first(ny):
                target = lax.rem(y + d, ny)
                source = part.at[core, pl.ds(x * per_x + target * per_y, per_y)]
                copies.append(copy(b, base[2] + d - 1, source, from_y.at[d - 1], y_peers[d - 1]))
        elif stage == 3:
            for d in farthest_first(nz):
                copies.append(copy(b, base[3] + d - 1, mine, from_z.at[d - 1], z_peers[d - 1]))
        elif stage == 4:
            whole = full.at[core, x, y]
            for d in farthest_first(ny):
                copies.append(copy(b, base[4] + d - 1, whole, whole, y_peers[d - 1]))
        elif stage == 5:
            whole = full.at[core, x]
            for d in farthest_first(nx):
                copies.append(copy(b, base[5] + d - 1, whole, whole, x_peers[d - 1]))
        else:
            copies = forwarded[b]
            return copies
        for each in copies:
            each.start()
        return copies

    forwarded = [[] for _ in range(nb)]

    def forward(b, d):
        chunk = batches[b][6].at[core, lax.rem(x + nx - d, nx)]
        forwarded[b].append(copy(b, base[6] + d, chunk, chunk, core_peer))
        forwarded[b][-1].start()

    def finish_stage(b, stage, copies):
        part, from_core, from_x, from_y, from_z, mine, full = batches[b]
        for d, each in zip(farthest_first(nx)[::-1], copies[::-1]):
            if stage == 5:
                each.wait_recv()
                forward(b, d)
        for each in copies:
            if stage != 5:
                each.wait_recv()
        if stage == 0:
            part[core] = part[core] + from_core[...]
        elif stage == 1:
            here = pl.ds(x * per_x, per_x)
            part[core, here] = part[core, here] + functools.reduce(
                jnp.add, [from_x[d] for d in range(nx - 1)]
            )
        elif stage == 2:
            here = pl.ds(x * per_x + y * per_y, per_y)
            mine[...] = part[core, here] + functools.reduce(
                jnp.add, [from_y[d] for d in range(ny - 1)]
            )
        elif stage == 3:
            full[core, x, y] = mine[...] + functools.reduce(
                jnp.add, [from_z[d] for d in range(nz - 1)]
            )

    started = [[] for _ in range(nb)]
    current = [None] * nb

    def begin(b, stage):
        current[b] = start_stage(b, stage)
        if stage == 5:
            forward(b, 0)
        started[b].append(current[b])

    def settle(b, keep):
        while len(started[b]) > keep:
            for each in started[b].pop(0):
                each.wait_send()

    def advance(b, stage):
        finish_stage(b, stage, current[b])
        if stage < 6:
            begin(b, stage + 1)
            settle(b, 2)

    def assemble(b):
        full = batches[b][6]
        columns = raw_ref.shape[2] // TILE_COLS
        for i in range(raw_ref.shape[1] // TILE_ROWS):
            for j in range(columns):
                tile = i * columns + j
                c, rest = divmod(tile, nx * per_x)
                x_, rest = divmod(rest, per_x)
                y_, t = divmod(rest, per_y)
                raw_ref[
                    b, i * TILE_ROWS : (i + 1) * TILE_ROWS, j * TILE_COLS : (j + 1) * TILE_COLS
                ] = full[c, x_, y_, t]

    for load in early:
        load.wait()
    for load in late:
        load.start()
    interpolate(0)
    pl.semaphore_wait(barrier, len(peers))
    tell(y_relay[0], ring(y_peers, 1))
    tell(z_relay[0], ring(z_peers, 1))
    begin(0, 0)
    advance(0, 0)
    interpolate(1)
    begin(1, 0)
    meet_y()
    meet_z(0)
    advance(1, 0)
    pl.semaphore_wait(y_relay[1], 2)
    advance(0, 1)
    meet_z(1)
    advance(1, 1)
    pl.semaphore_wait(z_relay[2], 2)
    for stage in range(2, 5):
        advance(0, stage)
        advance(1, stage)
    advance(0, 5)
    advance(0, 6)
    assemble(0)
    for load in late:
        load.wait()

    def receive():
        advance(1, 5)

    def receive_last():
        advance(1, 6)
        assemble(1)
        for b in range(nb):
            settle(b, 0)

    analyse(
        raw_ref,
        state_ref,
        noise_ref,
        tags_ref,
        values_ref,
        out_ref,
        rows_ref,
        m_ref,
        t_ref,
        receive,
        receive_last,
    )
    stores = [
        pltpu.make_async_copy(
            out_ref.at[pl.ds(i * piece, piece)],
            out_hbm.at[pl.ds(i * piece, piece)],
            load_sems.at[i],
        )
        for i in range(PIECES)
    ]
    for store in stores:
        store.start()
    for store in stores:
        store.wait()


def filter_call(ensemble, obs_blocks, obs_weights, comp_tags, obs_values, obs_noise):
    nx = NX
    ny = lax.axis_size("col")
    nz = lax.axis_size("row") // (2 * nx)
    batches, observations = obs_blocks.shape
    members = ensemble.shape[1]
    tiles = observations * members // (TILE_ROWS * TILE_COLS)
    per_x = tiles // (2 * nx)
    per_y = per_x // ny
    tile = (TILE_ROWS, TILE_COLS)
    one_batch = [
        pltpu.VMEM((2, tiles // 2, *tile), jnp.bfloat16),
        pltpu.VMEM((tiles // 2, *tile), jnp.bfloat16),
        pltpu.VMEM((nx - 1, per_x, *tile), jnp.bfloat16),
        pltpu.VMEM((ny - 1, per_y, *tile), jnp.bfloat16),
        pltpu.VMEM((nz - 1, per_y, *tile), jnp.bfloat16),
        pltpu.VMEM((per_y, *tile), jnp.bfloat16),
        pltpu.VMEM((2, nx, ny, per_y, *tile), jnp.bfloat16),
    ]
    copies = 2 * (nx + ny - 1) + nz - 1 + nx - 1
    weights = jnp.transpose(obs_weights, (0, 2, 1))
    operands = (ensemble, obs_blocks, weights, comp_tags, obs_values, obs_noise)
    square = pltpu.VMEM((observations, observations), jnp.float32)
    return pl.pallas_call(
        functools.partial(filter_kernel, nz, nx, ny),
        out_shape=jax.ShapeDtypeStruct(ensemble.shape, jnp.float32),
        in_specs=[pl.BlockSpec(memory_space=pltpu.HBM)] * len(operands),
        out_specs=pl.BlockSpec(memory_space=pltpu.HBM),
        scratch_shapes=[pltpu.VMEM(value.shape, value.dtype) for value in operands]
        + [
            pltpu.VMEM((observations, members), jnp.float32),
            pltpu.VMEM((batches, observations, members), jnp.bfloat16),
            square,
            square,
            pltpu.VMEM(ensemble.shape, jnp.float32),
            pltpu.SemaphoreType.DMA((len(operands) - 1 + PIECES,)),
            pltpu.SemaphoreType.DMA((batches, copies)),
            pltpu.SemaphoreType.DMA((batches, copies)),
        ]
        + [pltpu.SemaphoreType.REGULAR] * 5
        + one_batch * batches,
        compiler_params=pltpu.CompilerParams(
            collective_id=0, has_side_effects=True, vmem_limit_bytes=60 * 1024 * 1024
        ),
        cost_estimate=pl.CostEstimate(flops=10**10, bytes_accessed=10**7, transcendentals=0),
        name="ensemble_filter",
    )(*operands)


PANEL, SUB = 32, 16

def parts_of(value, count):
    parts = []
    for _ in range(count):
        part = value.astype(jnp.bfloat16)
        parts.append(part)
        value = value - part.astype(jnp.float32)
    return parts

def factor_inverse(m_ref, t_ref, meanwhile):
    panel, sub = PANEL, SUB
    size = m_ref.shape[0]
    lanes = lax.broadcasted_iota(jnp.int32, (panel, 128), 1)
    rows_of = lax.broadcasted_iota(jnp.int32, (panel, 128), 0)
    rows8 = lax.broadcasted_iota(jnp.int32, (8, 128), 0)
    for start in range(0, size, panel):
        tile, lane0 = start // 128, start % 128
        here = pl.ds(start, panel)
        block = m_ref[here, tile * 128 : tile * 128 + 128]
        wide = []
        for t in range(size // 128):
            part = block if t == tile else m_ref[here, t * 128 : t * 128 + 128]
            if t == tile:
                inside = (lanes >= lane0) & (lanes < lane0 + panel)
                part = jnp.where(inside, jnp.where(lanes - lane0 == rows_of, 1.0, 0.0), part)
            wide.append(part)
        wide.append(block)
        done = [[] for _ in wide]
        scales = []
        top = 0
        for s in range(0, panel, sub):
            columns = {
                j: jnp.broadcast_to(wide[-1][:, lane0 + j : lane0 + j + 1], wide[-1].shape)
                for j in range(s, s + sub)
            }
            for k in range(s, s + sub):
                if k - top == 8:
                    for i, part in enumerate(wide):
                        done[i].append(part[:8])
                        wide[i] = part[8:]
                    columns = {j: c[8:] for j, c in columns.items() if j >= k}
                    top += 8
                at = k - top
                if at == 0:
                    scale = jnp.zeros((8, 128), jnp.float32)
                pivot = columns[k][at : at + 1]
                inverse = 1.0 / pivot
                scale = jnp.where(rows8 == at, lax.rsqrt(pivot), scale)
                below = rows_of[: panel - top] > at
                multiple = jnp.where(below, columns[k] * inverse, 0.0)
                for j in range(k + 1, s + sub):
                    columns[j] = columns[j] - multiple * columns[j][at : at + 1]
                last = len(wide) if s + sub < panel else len(wide) - 1
                for i in range(last):
                    wide[i] = wide[i] - multiple * wide[i][at : at + 1]
                if at == 7:
                    scales.append(scale)
        for i, part in enumerate(wide):
            done[i].append(part)
        scale = jnp.concatenate(scales, axis=0)
        scaled = [jnp.concatenate(done[i], axis=0) * scale for i in range(size // 128)]
        for t in range(size // 128):
            kept = scaled[t]
            if t == tile:
                kept = jnp.where(lanes < lane0 + panel, kept, 0.0)
            elif t > tile:
                kept = jnp.zeros_like(kept)
            t_ref[here, t * 128 : t * 128 + 128] = kept
        after = start + panel
        if after < size:
            first = after // 128
            whole = jnp.concatenate(scaled, axis=1)
            p = parts_of(whole, 3)
            left = [p[0], p[0], p[1], p[1], p[0], p[2]]
            right = [p[0], p[1], p[0], p[1], p[2], p[0]]
            left = jnp.concatenate(left, axis=0)[:, first * 128 :]
            right = jnp.concatenate(right, axis=0)
            product = lax.dot_general(
                left, right, (((0,), (0,)), ((), ())), preferred_element_type=jnp.float32
            )[after - first * 128 :]
            for t in range(size // 128):
                old = m_ref[after:, t * 128 : t * 128 + 128]
                if t == tile:
                    at_lane = lax.broadcasted_iota(jnp.int32, old.shape, 1)
                    old = jnp.where((at_lane >= lane0) & (at_lane < lane0 + panel), 0.0, old)
                m_ref[after:, t * 128 : t * 128 + 128] = old - product[:, t * 128 : t * 128 + 128]
            meanwhile(start // panel)


def dot_nt(left, right):
    return lax.dot_general(
        left, right, (((1,), (1,)), ((), ())), preferred_element_type=jnp.float32
    )


def three_pass(dot, left, right):
    (left_high, left_low), (right_high, right_low) = left, right
    return dot(left_high, right_low) + dot(left_low, right_high) + dot(left_high, right_high)


def dot_nn(left, right):
    return jnp.dot(left, right, preferred_element_type=jnp.float32)


def two_pass(dot, pair, exact):
    return dot(pair[1], exact) + dot(pair[0], exact)


def analyse(
    raw_ref,
    state_ref,
    noise_ref,
    tags_ref,
    values_ref,
    out_ref,
    pending_ref,
    m_ref,
    t_ref,
    receive,
    receive_last,
):
    members = state_ref.shape[1]
    batches, observations = tags_ref.shape
    half = observations // 2
    share = 1.0 / (members - 1)
    variances = jnp.where(tags_ref[...] == 0, jnp.float32(0.5), jnp.float32(2.0))
    scales = jnp.sqrt(variances)
    shape = (observations, observations)
    diagonal = lax.broadcasted_iota(jnp.int32, shape, 0) == lax.broadcasted_iota(
        jnp.int32, shape, 1
    )

    def rotate(product, inverse):
        return split(three_pass(dot_nt, product, inverse))

    state_split = split(state_ref[...])
    found = {}
    for b in range(batches):
        observed = raw_ref[0] if b == 0 else pending_ref[...].astype(jnp.bfloat16)
        wide = observed.astype(jnp.float32)
        anomalies = split(wide - jnp.mean(wide, axis=1, keepdims=True))
        covariance = three_pass(dot_nt, anomalies, anomalies) * share
        m_ref[...] = covariance + jnp.where(diagonal, variances[b : b + 1], 0.0)

        def whiten(start, stop, b=b, observed=observed):
            factor = t_ref[start:stop, :stop]
            inverse = split(factor)
            scaled = split(factor * scales[b : b + 1, :stop])
            constant = jnp.sum(factor * values_ref[b : b + 1, :stop], axis=1, keepdims=True)
            white_innov = (
                two_pass(dot_nn, scaled, noise_ref[b, :stop])
                - two_pass(dot_nn, inverse, observed[:stop])
                + constant
            )
            return inverse, white_innov.astype(jnp.bfloat16)

        def turn_top(name):
            inverse, white_innov = found["top"]
            turned = rotate(tuple(part[:, :half] for part in found[name]), inverse)
            found[name + "_change"] = two_pass(dot_nn, turned, white_innov)

        def meanwhile(panel, b=b, anomalies=anomalies):
            if panel == 0 and b:
                state_ref[...] += found["change"]
            elif panel == 1:
                pair = split(state_ref[...]) if b else state_split
                found["state"] = split(three_pass(dot_nt, pair, anomalies) * share)
            elif panel == 3:
                found["top"] = whiten(0, half)
            elif panel == 5:
                turn_top("state")
            if b == 0 and panel == 2:
                receive()
            if b == 0 and panel == 5:
                receive_last()
                product = dot_nt(raw_ref[1], anomalies[1]) + dot_nt(raw_ref[1], anomalies[0])
                found["pending"] = split(product * share)
                turn_top("pending")

        factor_inverse(m_ref, t_ref, meanwhile)
        inverse, white_innov = whiten(half, observations)

        def last_change(name):
            turned = rotate(found[name], inverse)
            return found[name + "_change"] + two_pass(dot_nn, turned, white_innov)

        if b + 1 < batches:
            pending_ref[...] = raw_ref[1].astype(jnp.float32) + last_change("pending")
            found["change"] = last_change("state")
        else:
            out_ref[...] = state_ref[...] + last_change("state")


def solution(mesh):
    in_specs = (P(("row", "col"), None), P(), P(), P(), P(), P())
    out_specs = P(("row", "col"), None)
    return jax.shard_map(filter_call, mesh=mesh, in_specs=in_specs, out_specs=out_specs, check_vma=False)
```
